32 devices in a mesh: grp: 2 (over y), row: 4 (over x, core), col: 4 (over z).
Axes of the slice: x: 2, y: 2, z: 4, core: 2. Of those that a mesh axis runs over, the one named last changes fastest.
Arguments:
- tokens: bfloat16 [256, 4096], P(('grp', 'row', 'col')), parts along dimension 0, may hold values from -6 to 6
- dec_bias: bfloat16 [4096], replicated, may hold values from -3 to 3
- enc_rows: bfloat16 [4096, 4096], P(None, ('row', 'col')), may hold values from -0.09375 to 0.09375
- bias_rows: bfloat16 [4096], P(('row', 'col')), may hold values from -3 to 3
- enc_cols: bfloat16 [4096, 16384], P(None, ('col', 'row')), may hold values from -0.09375 to 0.09375
- bias_cols: bfloat16 [16384], P(('col', 'row')), may hold values from -3 to 3
Outputs:
- slab: bfloat16 [8192, 16384], P(('grp', 'row'), 'col'), parts along dimension 0
The draws below stay inside these ranges and needn't reach their ends.
There are 2 independent parts, one for each index of `grp`. The reference program is written for one: setup_inputs(seed, part) draws one part's arguments, and reference() takes and returns one part's arrays. A program takes and returns all parts, laid end to end along the dimension named above; an argument that names none is the same for every part. Nothing has to cross between parts.
All inputs are finite; a program needn't handle non-finite values.
Results may differ from the reference program's by a relative error of at most 0.0034.
Values may be sent and summed in bfloat16 or wider, within the bound.
A program may use at most 64 MiB of HBM per device.

```python
import jax
import jax.numpy as jnp
from jax import lax

D = 4096
TOKENS = 128
LR = 4096
LC = 16384


def steps_of(own_key, extent, cuts, low, top_value):
    loudness = 1.0
    for axis_at, shards_of in cuts:
        steps = jax.random.uniform(jax.random.fold_in(jax.random.fold_in(own_key, 6), axis_at), (shards_of,), jnp.float32, low / len(cuts), top_value / len(cuts))
        loudness = loudness * jnp.repeat(jnp.exp(steps), extent[axis_at] // shards_of).reshape((-1,) + (1,) * (len(extent) - 1 - axis_at))
    return loudness


def centred(stream_key, shape, spread, reach, split=(), held_as=jnp.bfloat16):
    loudness = steps_of(stream_key, shape, split, -0.22, 0.18) if split else 1.0
    values = jax.random.normal(stream_key, shape, jnp.float32) * spread * loudness
    return jnp.minimum(jnp.maximum(values, -reach), reach).astype(held_as)


def setup_inputs(seed: int = 0, part: int = 0) -> dict:
    splits = jax.random.split(jax.random.key(seed), 7)
    part_keys = jax.random.split(jax.random.fold_in(splits[6], part), 7)
    return {
        "tokens": centred(part_keys[0], (TOKENS, D), 1.0, 6.0, ((0, 16),)),
        "dec_bias": centred(splits[1], (D,), 0.5, 3.0),
        "enc_rows": centred(splits[2], (D, LR), D ** -0.5, 0.09375, ((1, 16),)),
        "bias_rows": centred(splits[3], (LR,), 0.5, 3.0, ((0, 16),)),
        "enc_cols": centred(splits[4], (D, LC), D ** -0.5, 0.09375, ((1, 16),)),
        "bias_cols": centred(splits[5], (LC,), 0.5, 3.0, ((0, 16),)),
    }


def reference(tokens, dec_bias, enc_rows, bias_rows, enc_cols, bias_cols):
    centered = (tokens.astype(jnp.float32) - dec_bias.astype(jnp.float32)).astype(jnp.bfloat16)
    row_pre = jnp.dot(centered, enc_rows, preferred_element_type=jnp.float32) + bias_rows.astype(jnp.float32)
    row_codes = jax.nn.relu(row_pre).astype(jnp.bfloat16)
    col_pre = jnp.dot(centered, enc_cols, preferred_element_type=jnp.float32) + bias_cols.astype(jnp.float32)
    col_codes = jax.nn.relu(col_pre).astype(jnp.bfloat16)
    total = lax.dot_general(row_codes, col_codes, (((0,), (0,)), ((), ())), preferred_element_type=jnp.float32)
    return (total / TOKENS).astype(jnp.bfloat16)
```

```python
import functools

import jax
import jax.numpy as jnp
from jax import lax
from jax.experimental import pallas as pl
from jax.experimental.pallas import tpu as pltpu
from jax.sharding import PartitionSpec as P

MESH = pl.DeviceIdType.MESH
CORES = 2
CHUNKS = 4
PIECE = 256


def gather_encode(
    n_row, n_col, tokens, dec_bias, enc_rows, bias_rows, enc_cols, bias_cols,
    rows_out, cols_out,
    tok, w_rows, w_cols, acc_rows, acc_cols, w_sem, own_sem,
    z_send, z_recv, x_send, x_recv, s_send, s_recv,
    rz_send, rz_recv, cx_send, cx_recv, cs_send, cs_recv,
):
    n_x = n_row // CORES
    r, c = lax.axis_index("row"), lax.axis_index("col")
    x, k = r // CORES, r % CORES
    other = 1 - k
    sibling = {"row": x * CORES + other, "col": c}
    block, width = tokens.shape
    part = width // CHUNKS
    n_piece, n_tok, piece = cols_out.shape[1:]

    def z_peer(s):
        return lax.rem(c + s, n_col)

    def x_peer(t):
        return {"row": lax.rem(x + t, n_x) * CORES + k, "col": c}

    def cols(d):
        return pl.ds(d * part, part)

    w_copies = []
    own_copies = []
    for d in range(CHUNKS):
        own = pltpu.make_async_copy(
            tokens.at[:, cols(d)], tok.at[k, x, c, :, cols(d)], own_sem.at[d]
        )
        own.start()
        own_copies.append(own)
    for d in range(CHUNKS):
        pair = (
            pltpu.make_async_copy(enc_rows.at[cols(d)], w_rows.at[cols(d)], w_sem.at[d, 0]),
            pltpu.make_async_copy(enc_cols.at[cols(d)], w_cols.at[cols(d)], w_sem.at[d, 1]),
        )
        for copy in pair:
            copy.start()
        w_copies.append(pair)

    barrier = pltpu.get_barrier_semaphore()
    for s in range(1, n_col):
        pl.semaphore_signal(barrier, inc=1, device_id={"row": r, "col": z_peer(s)}, device_id_type=MESH)
    for t in range(1, n_x):
        pl.semaphore_signal(barrier, inc=1, device_id=x_peer(t), device_id_type=MESH)
    pl.semaphore_signal(barrier, inc=1, device_id=sibling, device_id_type=MESH)
    pl.semaphore_wait(barrier, n_col - 1 + n_x - 1 + 1)

    def to_x(src, dst_c, d, s):
        for t in range(1, n_x):
            pltpu.make_async_remote_copy(
                src_ref=src, dst_ref=tok.at[k, x, dst_c, :, cols(d)],
                send_sem=x_send.at[d], recv_sem=x_recv.at[d, t, s],
                device_id=x_peer(t), device_id_type=MESH,
            ).start()

    def to_sibling(src, dst_x, dst_c, d):
        pltpu.make_async_remote_copy(
            src_ref=src, dst_ref=tok.at[k, dst_x, dst_c, :, cols(d)],
            send_sem=s_send.at[d], recv_sem=s_recv.at[d],
            device_id=sibling, device_id_type=MESH,
        ).start()

    for d in range(CHUNKS):
        src = tokens.at[:, cols(d)]
        for s in range(1, n_col):
            pltpu.make_async_remote_copy(
                src_ref=src, dst_ref=tok.at[k, x, c, :, cols(d)],
                send_sem=z_send.at[d], recv_sem=z_recv.at[d, s],
                device_id={"row": r, "col": z_peer(s)}, device_id_type=MESH,
            ).start()
        to_x(src, c, d, 0)
        to_sibling(src, x, c, d)

    def forward_z(d):
        for s in range(1, n_col):
            from_c = lax.rem(c + n_col - s, n_col)
            landed = tok.at[k, x, from_c, :, cols(d)]
            pltpu.make_async_copy(landed, landed, z_recv.at[d, s]).wait()
            to_x(landed, from_c, d, s)
            to_sibling(landed, x, from_c, d)

    def forward_x(d):
        for s in range(n_col):
            from_c = lax.rem(c + n_col - s, n_col)
            for t in range(1, n_x):
                from_x = lax.rem(x + n_x - t, n_x)
                landed = tok.at[k, from_x, from_c, :, cols(d)]
                pltpu.make_async_copy(landed, landed, x_recv.at[d, t, s]).wait()
                to_sibling(landed, from_x, from_c, d)

    def centered(d):
        landed = tok.at[other, :, :, :, cols(d)]
        pltpu.make_async_copy(landed, landed, s_recv.at[d]).wait()
        own_copies[d].wait()
        for copy in w_copies[d]:
            copy.wait()
        raw = tok[:, :, :, :, cols(d)].astype(jnp.float32).reshape(n_tok, part)
        return (raw - dec_bias[:, cols(d)].astype(jnp.float32)).astype(jnp.bfloat16)

    def dot(a, b):
        return jnp.dot(a, b, preferred_element_type=jnp.float32)

    forward_z(0)
    for d in range(CHUNKS):
        if d + 1 < CHUNKS:
            forward_z(d + 1)
        forward_x(d)
        cent = centered(d)
        if d + 1 < CHUNKS:
            new_rows = dot(cent, w_rows[cols(d)])
            acc_rows[...] = new_rows if d == 0 else acc_rows[...] + new_rows
            for p in range(n_piece):
                at = pl.ds(p * piece, piece)
                new = dot(cent, w_cols[cols(d), at])
                acc_cols[:, at] = new if d == 0 else acc_cols[:, at] + new

    last = CHUNKS - 1

    def finish(acc, weight, bias):
        total = dot(cent, weight)
        if last:
            total = total + acc
        return jax.nn.relu(total + bias.astype(jnp.float32)).astype(jnp.bfloat16)

    row_codes = finish(acc_rows[...], w_rows[cols(last)], bias_rows[...])
    rows_out[c] = row_codes.astype(jnp.float32).T.astype(jnp.bfloat16)
    row_copies = []
    for s in range(1, n_col):
        copy = pltpu.make_async_remote_copy(
            src_ref=rows_out.at[c], dst_ref=rows_out.at[c],
            send_sem=rz_send.at[s], recv_sem=rz_recv.at[s],
            device_id={"row": r, "col": z_peer(s)}, device_id_type=MESH,
        )
        copy.start()
        row_copies.append(copy)

    def codes_to_sibling(src_r, t, p):
        copy = pltpu.make_async_remote_copy(
            src_ref=cols_out.at[src_r, p], dst_ref=cols_out.at[src_r, p],
            send_sem=cs_send.at[t, p], recv_sem=cs_recv.at[t, p],
            device_id=sibling, device_id_type=MESH,
        )
        copy.start()
        return copy

    x_copies, s_copies = [], []
    for p in range(n_piece):
        at = pl.ds(p * piece, piece)
        cols_out[r, p] = finish(acc_cols[:, at], w_cols[cols(last), at], bias_cols[:, at])
        for t in range(1, n_x):
            copy = pltpu.make_async_remote_copy(
                src_ref=cols_out.at[r, p], dst_ref=cols_out.at[r, p],
                send_sem=cx_send.at[t, p], recv_sem=cx_recv.at[t, p],
                device_id=x_peer(t), device_id_type=MESH,
            )
            copy.start()
            x_copies.append(copy)
        s_copies.append(codes_to_sibling(r, 0, p))
    for p in range(n_piece):
        for t in range(1, n_x):
            from_r = lax.rem(x + n_x - t, n_x) * CORES + k
            landed = cols_out.at[from_r, p]
            pltpu.make_async_copy(landed, landed, cx_recv.at[t, p]).wait()
            s_copies.append(codes_to_sibling(from_r, t, p))

    for d in range(CHUNKS):
        some = tok.at[0, 0, pl.ds(0, n_col - 1), :, cols(d)]
        pltpu.make_async_copy(some, some, z_send.at[d]).wait()
        some = tok.at[0, pl.ds(0, n_x - 1), :, :, cols(d)]
        pltpu.make_async_copy(some, some, x_send.at[d]).wait()
        some = tok.at[0, :, :, :, cols(d)]
        pltpu.make_async_copy(some, some, s_send.at[d]).wait()
    for copy in row_copies:
        copy.wait()
    for copy in x_copies:
        copy.wait_send()
    for copy in s_copies:
        copy.wait()


def slab_kernel(scale, rows, cols, out):
    n_piece, _, piece = cols.shape[1:]
    left = rows[...].reshape(-1, rows.shape[2])
    for p in range(n_piece):
        total = jnp.dot(left, cols[0, p], preferred_element_type=jnp.float32)
        out[:, p * piece:(p + 1) * piece] = (total * scale).astype(jnp.bfloat16)


def on_device(n_row, n_col, tokens, dec_bias, enc_rows, bias_rows, enc_cols, bias_cols):
    block, width = tokens.shape
    n_tok = block * n_row * n_col
    n_x = n_row // CORES
    row_width, col_width = enc_rows.shape[1], enc_cols.shape[1]
    piece = min(PIECE, col_width)
    n_piece = col_width // piece
    dma = pltpu.SemaphoreType.DMA
    vmem = pl.BlockSpec(memory_space=pltpu.VMEM)
    anywhere = pl.BlockSpec(memory_space=pl.ANY)
    rows, cols = pl.pallas_call(
        functools.partial(gather_encode, n_row, n_col),
        out_shape=(
            jax.ShapeDtypeStruct((n_col, row_width, n_tok), jnp.bfloat16),
            jax.ShapeDtypeStruct((n_row, n_piece, n_tok, piece), jnp.bfloat16),
        ),
        in_specs=[anywhere, vmem, anywhere, vmem, anywhere, vmem],
        out_specs=(vmem, vmem),
        scratch_shapes=[
            pltpu.VMEM((CORES, n_x, n_col, block, width), jnp.bfloat16),
            pltpu.VMEM((width, row_width), jnp.bfloat16),
            pltpu.VMEM((width, col_width), jnp.bfloat16),
            pltpu.VMEM((n_tok, row_width), jnp.float32),
            pltpu.VMEM((n_tok, col_width), jnp.float32),
            dma((CHUNKS, 2)),
            dma((CHUNKS,)),
            dma((CHUNKS,)),
            dma((CHUNKS, n_col)),
            dma((CHUNKS,)),
            dma((CHUNKS, n_x, n_col)),
            dma((CHUNKS,)),
            dma((CHUNKS,)),
            dma((n_col,)),
            dma((n_col,)),
            dma((n_x, n_piece)),
            dma((n_x, n_piece)),
            dma((n_x, n_piece)),
            dma((n_x, n_piece)),
        ],
        compiler_params=pltpu.CompilerParams(
            collective_id=0, has_side_effects=True, vmem_limit_bytes=56 * 2**20
        ),
        name="gather_encode",
    )(
        tokens, dec_bias.reshape(1, -1), enc_rows, bias_rows.reshape(1, -1),
        enc_cols, bias_cols.reshape(1, -1),
    )
    return pl.pallas_call(
        functools.partial(slab_kernel, 1.0 / n_tok),
        out_shape=jax.ShapeDtypeStruct((n_col * row_width, n_row * col_width), jnp.bfloat16),
        grid=(n_row,),
        in_specs=[
            pl.BlockSpec((n_col, row_width, n_tok), lambda i: (0, 0, 0)),
            pl.BlockSpec((1, n_piece, n_tok, piece), lambda i: (i, 0, 0, 0)),
        ],
        out_specs=pl.BlockSpec((n_col * row_width, col_width), lambda i: (0, i)),
        compiler_params=pltpu.CompilerParams(vmem_limit_bytes=40 * 2**20),
        name="slab",
    )(rows, cols)


def solution(mesh):
    in_specs = (
        P(("grp", "row", "col"), None),
        P(),
        P(None, ("row", "col")),
        P(("row", "col")),
        P(None, ("col", "row")),
        P(("col", "row")),
    )
    out_specs = P(("grp", "row"), "col")
    return jax.shard_map(
        functools.partial(on_device, mesh.shape["row"], mesh.shape["col"]),
        mesh=mesh, in_specs=in_specs, out_specs=out_specs, check_vma=False,
    )
```

```python
import functools

import jax
import jax.numpy as jnp
from jax import lax
from jax.experimental import pallas as pl
from jax.experimental.pallas import tpu as pltpu
from jax.sharding import PartitionSpec as P

MESH = pl.DeviceIdType.MESH
CORES = 2
PIECE = 256


def gather_encode(
    n_row, n_col, tokens, dec_bias, enc_rows, bias_rows, enc_cols, bias_cols,
    rows_out, cols_out,
    tok, cent, w_rows, w_cols, shift, b_rows, b_cols, w_sem, b_sem, own_sem,
    z_send, z_recv, x_send, x_recv, s_send, s_recv,
    rz_send, rz_recv, cx_send, cx_recv, cs_send, cs_recv,
):
    n_x = n_row // CORES
    r, c = lax.axis_index("row"), lax.axis_index("col")
    x, k = r // CORES, r % CORES
    other = 1 - k
    sibling = {"row": x * CORES + other, "col": c}
    n_piece, n_tok, piece = cols_out.shape[1:]

    def z_peer(s):
        return {"row": r, "col": lax.rem(c + s, n_col)}

    def x_peer(t):
        return {"row": lax.rem(x + t, n_x) * CORES + k, "col": c}

    def from_c(s):
        return lax.rem(c + n_col - s, n_col)

    def from_x(t):
        return lax.rem(x + n_x - t, n_x)

    def local(src, dst, sem):
        copy = pltpu.make_async_copy(src, dst, sem)
        copy.start()
        return copy

    def remote(src, dst, send_sem, recv_sem, device):
        copy = pltpu.make_async_remote_copy(
            src_ref=src, dst_ref=dst, send_sem=send_sem, recv_sem=recv_sem,
            device_id=device, device_id_type=MESH,
        )
        copy.start()
        return copy

    def landed(ref, sem):
        pltpu.make_async_copy(ref, ref, sem).wait()

    barrier = pltpu.get_barrier_semaphore()
    for s in range(1, n_col):
        pl.semaphore_signal(barrier, inc=1, device_id=z_peer(s), device_id_type=MESH)
    for t in range(1, n_x):
        pl.semaphore_signal(barrier, inc=1, device_id=x_peer(t), device_id_type=MESH)
    pl.semaphore_signal(barrier, inc=1, device_id=sibling, device_id_type=MESH)

    own = local(tokens, tok.at[k, x, c], own_sem)
    b_copies = [
        local(dec_bias, shift, b_sem.at[0]),
        local(bias_rows, b_rows, b_sem.at[1]),
        local(bias_cols, b_cols, b_sem.at[2]),
    ]
    pl.semaphore_wait(barrier, n_col - 1 + n_x - 1 + 1)

    sent = []
    for s in range(1, n_col):
        sent.append(remote(tokens, tok.at[k, x, c], z_send.at[s], z_recv.at[s], z_peer(s)))
    for t in range(1, n_x):
        sent.append(remote(tokens, tok.at[k, x, c], x_send.at[t, 0], x_recv.at[t, 0], x_peer(t)))
    w_copies = [
        local(enc_cols, w_cols, w_sem.at[0]),
        local(enc_rows, w_rows, w_sem.at[1]),
    ]
    for s in range(1, n_col):
        block = tok.at[k, x, from_c(s)]
        landed(block, z_recv.at[s])
        for t in range(1, n_x):
            sent.append(remote(block, block, x_send.at[t, s], x_recv.at[t, s], x_peer(t)))
    own.wait()
    sent.append(remote(tok.at[k, x], tok.at[k, x], s_send.at[0], s_recv.at[0], sibling))
    for copy in b_copies:
        copy.wait()
    shift_row = shift[...].astype(jnp.float32).reshape(1, -1)

    def centre(kk, xx):
        raw = tok[kk, xx].astype(jnp.float32).reshape(cent.shape[2:])
        cent[kk, xx] = (raw - shift_row).astype(jnp.bfloat16)

    centre(k, x)
    for t in range(1, n_x):
        for s in range(n_col):
            landed(tok.at[k, from_x(t), from_c(s)], x_recv.at[t, s])
        plane = tok.at[k, from_x(t)]
        sent.append(remote(plane, plane, s_send.at[t], s_recv.at[t], sibling))
    for t in range(1, n_x):
        centre(k, from_x(t))
    for t in range(n_x):
        landed(tok.at[other, from_x(t)], s_recv.at[t])
        centre(other, from_x(t))

    def encode(weight, bias):
        total = jnp.dot(
            cent[...].reshape(n_tok, -1), weight, preferred_element_type=jnp.float32
        )
        return jax.nn.relu(total + bias).astype(jnp.bfloat16)

    row_bias = b_rows[...].astype(jnp.float32).reshape(1, -1)
    col_bias = b_cols[...].astype(jnp.float32).reshape(1, -1)
    w_copies[0].wait()
    for p in range(n_piece):
        at = slice(p * piece, (p + 1) * piece)
        cols_out[r, p] = encode(w_cols[:, at], col_bias[:, at])
        mine = cols_out.at[r, p]
        for t in range(1, n_x):
            sent.append(remote(mine, mine, cx_send.at[t, p], cx_recv.at[t, p], x_peer(t)))
        sent.append(remote(mine, mine, cs_send.at[0, p], cs_recv.at[0, p], sibling))
        if p == 0:
            w_copies[1].wait()
            rows_out[c] = encode(w_rows[...], row_bias).astype(jnp.float32).T.astype(jnp.bfloat16)
            for s in range(1, n_col):
                sent.append(
                    remote(rows_out.at[c], rows_out.at[c], rz_send.at[s], rz_recv.at[s], z_peer(s))
                )
    for p in range(n_piece):
        for t in range(1, n_x):
            theirs = cols_out.at[from_x(t) * CORES + k, p]
            landed(theirs, cx_recv.at[t, p])
            sent.append(remote(theirs, theirs, cs_send.at[t, p], cs_recv.at[t, p], sibling))

    for s in range(1, n_col):
        landed(rows_out.at[from_c(s)], rz_recv.at[s])
    for t in range(n_x):
        for p in range(n_piece):
            landed(cols_out.at[from_x(t) * CORES + other, p], cs_recv.at[t, p])
    for copy in sent:
        copy.wait_send()


def slab_kernel(scale, rows, cols, out):
    n_piece, _, piece = cols.shape[1:]
    left = rows[...].reshape(-1, rows.shape[2])
    for p in range(n_piece):
        total = jnp.dot(left, cols[0, p], preferred_element_type=jnp.float32)
        out[:, p * piece:(p + 1) * piece] = (total * scale).astype(jnp.bfloat16)


def on_device(n_row, n_col, tokens, dec_bias, enc_rows, bias_rows, enc_cols, bias_cols):
    block, width = tokens.shape
    n_tok = block * n_row * n_col
    n_x = n_row // CORES
    row_width, col_width = enc_rows.shape[1], enc_cols.shape[1]
    piece = min(PIECE, col_width)
    n_piece = col_width // piece
    dma = pltpu.SemaphoreType.DMA
    vmem = pl.BlockSpec(memory_space=pltpu.VMEM)
    anywhere = pl.BlockSpec(memory_space=pl.ANY)
    rows, cols = pl.pallas_call(
        functools.partial(gather_encode, n_row, n_col),
        out_shape=(
            pltpu.VMEM((n_col, row_width, n_tok), jnp.bfloat16),
            pltpu.VMEM((n_row, n_piece, n_tok, piece), jnp.bfloat16),
        ),
        in_specs=[anywhere] * 6,
        out_specs=(vmem, vmem),
        scratch_shapes=[
            pltpu.VMEM((CORES, n_x, n_col, block, width), jnp.bfloat16),
            pltpu.VMEM((CORES, n_x, n_col * block, width), jnp.bfloat16),
            pltpu.VMEM((width, row_width), jnp.bfloat16),
            pltpu.VMEM((width, col_width), jnp.bfloat16),
            pltpu.VMEM((width,), jnp.bfloat16),
            pltpu.VMEM((row_width,), jnp.bfloat16),
            pltpu.VMEM((col_width,), jnp.bfloat16),
            dma((2,)),
            dma((3,)),
            dma,
            dma((n_col,)),
            dma((n_col,)),
            dma((n_x, n_col)),
            dma((n_x, n_col)),
            dma((n_x,)),
            dma((n_x,)),
            dma((n_col,)),
            dma((n_col,)),
            dma((n_x, n_piece)),
            dma((n_x, n_piece)),
            dma((n_x, n_piece)),
            dma((n_x, n_piece)),
        ],
        compiler_params=pltpu.CompilerParams(
            collective_id=0, has_side_effects=True, vmem_limit_bytes=36 * 2**20
        ),
        name="gather_encode",
    )(
        tokens, dec_bias, enc_rows, bias_rows, enc_cols, bias_cols
    )
    return pl.pallas_call(
        functools.partial(slab_kernel, 1.0 / n_tok),
        out_shape=jax.ShapeDtypeStruct((n_col * row_width, n_row * col_width), jnp.bfloat16),
        grid=(n_row,),
        in_specs=[
            pl.BlockSpec((n_col, row_width, n_tok), lambda i: (0, 0, 0)),
            pl.BlockSpec((1, n_piece, n_tok, piece), lambda i: (i, 0, 0, 0)),
        ],
        out_specs=pl.BlockSpec((n_col * row_width, col_width), lambda i: (0, i)),
        compiler_params=pltpu.CompilerParams(vmem_limit_bytes=40 * 2**20),
        name="slab",
    )(rows, cols)


def solution(mesh):
    in_specs = (
        P(("grp", "row", "col"), None),
        P(),
        P(None, ("row", "col")),
        P(("row", "col")),
        P(None, ("col", "row")),
        P(("col", "row")),
    )
    out_specs = P(("grp", "row"), "col")
    return jax.shard_map(
        functools.partial(on_device, mesh.shape["row"], mesh.shape["col"]),
        mesh=mesh, in_specs=in_specs, out_specs=out_specs, check_vma=False,
    )
```

```python
import functools

import jax
import jax.numpy as jnp
from jax import lax
from jax.experimental import pallas as pl
from jax.experimental.pallas import tpu as pltpu
from jax.sharding import PartitionSpec as P

MESH = pl.DeviceIdType.MESH
CORES = 2
PIECE = 256


def gather_encode(
    n_row, n_col, tokens, dec_bias, enc_rows, bias_rows, enc_cols, bias_cols,
    rows_out, cols_out,
    tok, cent, w_rows, w_cols, shift, b_rows, b_cols, w_sem, b_sem, own_sem,
    z_send, z_recv, x_send, x_recv, s_send, s_recv,
    rz_send, rz_recv, cx_send, cx_recv, cs_send, cs_recv,
):
    n_x = n_row // CORES
    r, c = lax.axis_index("row"), lax.axis_index("col")
    x, k = r // CORES, r % CORES
    other = 1 - k
    sibling = {"row": x * CORES + other, "col": c}
    n_piece, n_tok, piece = cols_out.shape[1:]

    def z_peer(s):
        return {"row": r, "col": lax.rem(c + s, n_col)}

    def x_peer(t):
        return {"row": lax.rem(x + t, n_x) * CORES + k, "col": c}

    def from_c(s):
        return lax.rem(c + n_col - s, n_col)

    def from_x(t):
        return lax.rem(x + n_x - t, n_x)

    def local(src, dst, sem):
        copy = pltpu.make_async_copy(src, dst, sem)
        copy.start()
        return copy

    def remote(src, dst, send_sem, recv_sem, device):
        copy = pltpu.make_async_remote_copy(
            src_ref=src, dst_ref=dst, send_sem=send_sem, recv_sem=recv_sem,
            device_id=device, device_id_type=MESH,
        )
        copy.start()
        return copy

    def landed(ref, sem):
        pltpu.make_async_copy(ref, ref, sem).wait()

    barrier = pltpu.get_barrier_semaphore()
    for s in range(1, n_col):
        pl.semaphore_signal(barrier, inc=1, device_id=z_peer(s), device_id_type=MESH)
    for t in range(1, n_x):
        pl.semaphore_signal(barrier, inc=1, device_id=x_peer(t), device_id_type=MESH)
    pl.semaphore_signal(barrier, inc=1, device_id=sibling, device_id_type=MESH)

    own = local(tokens, tok.at[k, x, c], own_sem)
    b_copies = [
        local(dec_bias, shift, b_sem.at[0]),
        local(bias_rows, b_rows, b_sem.at[1]),
        local(bias_cols, b_cols, b_sem.at[2]),
    ]
    w_copies = [
        local(enc_cols, w_cols, w_sem.at[0]),
        local(enc_rows, w_rows, w_sem.at[1]),
    ]
    pl.semaphore_wait(barrier, n_col - 1 + n_x - 1 + 1)

    sent = []
    for s in range(1, n_col):
        sent.append(remote(tokens, tok.at[k, x, c], z_send.at[s], z_recv.at[s], z_peer(s)))
    for t in range(1, n_x):
        sent.append(remote(tokens, tok.at[k, x, c], x_send.at[t, 0], x_recv.at[t, 0], x_peer(t)))
    for s in range(1, n_col):
        block = tok.at[k, x, from_c(s)]
        landed(block, z_recv.at[s])
        for t in range(1, n_x):
            sent.append(remote(block, block, x_send.at[t, s], x_recv.at[t, s], x_peer(t)))
    own.wait()
    sent.append(remote(tok.at[k, x], tok.at[k, x], s_send.at[0], s_recv.at[0], sibling))
    for copy in b_copies:
        copy.wait()
    shift_row = shift[...].astype(jnp.float32).reshape(1, -1)

    def centre(kk, xx):
        raw = tok[kk, xx].astype(jnp.float32).reshape(cent.shape[2:])
        cent[kk, xx] = (raw - shift_row).astype(jnp.bfloat16)

    centre(k, x)
    for t in range(1, n_x):
        for s in range(n_col):
            landed(tok.at[k, from_x(t), from_c(s)], x_recv.at[t, s])
        plane = tok.at[k, from_x(t)]
        sent.append(remote(plane, plane, s_send.at[t], s_recv.at[t], sibling))
    for t in range(1, n_x):
        centre(k, from_x(t))
    for t in range(n_x):
        landed(tok.at[other, from_x(t)], s_recv.at[t])
        centre(other, from_x(t))

    def encode(weight, bias):
        total = jnp.dot(
            cent[...].reshape(n_tok, -1), weight, preferred_element_type=jnp.float32
        )
        return jax.nn.relu(total + bias).astype(jnp.bfloat16)

    row_bias = b_rows[...].astype(jnp.float32).reshape(1, -1)
    col_bias = b_cols[...].astype(jnp.float32).reshape(1, -1)
    w_copies[0].wait()
    for p in range(n_piece):
        at = slice(p * piece, (p + 1) * piece)
        cols_out[r, p] = encode(w_cols[:, at], col_bias[:, at])
        mine = cols_out.at[r, p]
        for t in range(1, n_x):
            sent.append(remote(mine, mine, cx_send.at[t, p], cx_recv.at[t, p], x_peer(t)))
        sent.append(remote(mine, mine, cs_send.at[0, p], cs_recv.at[0, p], sibling))
        if p == 0:
            w_copies[1].wait()
            rows_out[c] = encode(w_rows[...], row_bias).astype(jnp.float32).T.astype(jnp.bfloat16)
            for s in range(1, n_col):
                sent.append(
                    remote(rows_out.at[c], rows_out.at[c], rz_send.at[s], rz_recv.at[s], z_peer(s))
                )
    for p in range(n_piece):
        for t in range(1, n_x):
            theirs = cols_out.at[from_x(t) * CORES + k, p]
            landed(theirs, cx_recv.at[t, p])
            sent.append(remote(theirs, theirs, cs_send.at[t, p], cs_recv.at[t, p], sibling))

    for s in range(1, n_col):
        landed(rows_out.at[from_c(s)], rz_recv.at[s])
    for t in range(n_x):
        for p in range(n_piece):
            landed(cols_out.at[from_x(t) * CORES + other, p], cs_recv.at[t, p])
    for copy in sent:
        copy.wait_send()


def slab_kernel(scale, rows, cols, out, held, sem):
    n_row, n_piece, _, piece = cols.shape
    left = rows[...].reshape(-1, rows.shape[2])

    def copy(i, p):
        at = pl.ds(pl.multiple_of((i * n_piece + p) * piece, piece), piece)
        return pltpu.make_async_copy(held.at[i, p], out.at[:, at], sem.at[i, p])

    @pl.loop(0, n_row)
    def _(i):
        for p in range(n_piece):
            total = jnp.dot(left, cols[i, p], preferred_element_type=jnp.float32)
            held[i, p] = (total * scale).astype(jnp.bfloat16)
            copy(i, p).start()

    @pl.loop(0, n_row)
    def _(i):
        for p in range(n_piece):
            copy(i, p).wait()


def on_device(n_row, n_col, tokens, dec_bias, enc_rows, bias_rows, enc_cols, bias_cols):
    block, width = tokens.shape
    n_tok = block * n_row * n_col
    n_x = n_row // CORES
    row_width, col_width = enc_rows.shape[1], enc_cols.shape[1]
    piece = min(PIECE, col_width)
    n_piece = col_width // piece
    out_bytes = 2 * n_tok * (n_col * row_width + n_row * col_width)
    dma = pltpu.SemaphoreType.DMA
    vmem = pl.BlockSpec(memory_space=pltpu.VMEM)
    anywhere = pl.BlockSpec(memory_space=pltpu.HBM)
    rows, cols = pl.pallas_call(
        functools.partial(gather_encode, n_row, n_col),
        out_shape=(
            pltpu.VMEM((n_col, row_width, n_tok), jnp.bfloat16),
            pltpu.VMEM((n_row, n_piece, n_tok, piece), jnp.bfloat16),
        ),
        in_specs=[anywhere] * 6,
        out_specs=(vmem, vmem),
        scratch_shapes=[
            pltpu.VMEM((CORES, n_x, n_col, block, width), jnp.bfloat16),
            pltpu.VMEM((CORES, n_x, n_col * block, width), jnp.bfloat16),
            pltpu.VMEM((width, row_width), jnp.bfloat16),
            pltpu.VMEM((width, col_width), jnp.bfloat16),
            pltpu.VMEM((width,), jnp.bfloat16),
            pltpu.VMEM((row_width,), jnp.bfloat16),
            pltpu.VMEM((col_width,), jnp.bfloat16),
            dma((2,)),
            dma((3,)),
            dma,
            dma((n_col,)),
            dma((n_col,)),
            dma((n_x, n_col)),
            dma((n_x, n_col)),
            dma((n_x,)),
            dma((n_x,)),
            dma((n_col,)),
            dma((n_col,)),
            dma((n_x, n_piece)),
            dma((n_x, n_piece)),
            dma((n_x, n_piece)),
            dma((n_x, n_piece)),
        ],
        compiler_params=pltpu.CompilerParams(
            collective_id=0, has_side_effects=True, vmem_limit_bytes=57 * 2**20 - out_bytes
        ),
        name="gather_encode",
    )(
        tokens, dec_bias, enc_rows, bias_rows, enc_cols, bias_cols
    )
    return pl.pallas_call(
        functools.partial(slab_kernel, 1.0 / n_tok),
        out_shape=jax.ShapeDtypeStruct((n_col * row_width, n_row * col_width), jnp.bfloat16),
        in_specs=[vmem, vmem],
        out_specs=anywhere,
        scratch_shapes=[
            pltpu.VMEM((n_row, n_piece, n_col * row_width, piece), jnp.bfloat16),
            dma((n_row, n_piece)),
        ],
        compiler_params=pltpu.CompilerParams(vmem_limit_bytes=40 * 2**20),
        name="slab",
    )(rows, cols)


def solution(mesh):
    in_specs = (
        P(("grp", "row", "col"), None),
        P(),
        P(None, ("row", "col")),
        P(("row", "col")),
        P(None, ("col", "row")),
        P(("col", "row")),
    )
    out_specs = P(("grp", "row"), "col")
    return jax.shard_map(
        functools.partial(on_device, mesh.shape["row"], mesh.shape["col"]),
        mesh=mesh, in_specs=in_specs, out_specs=out_specs, check_vma=False,
    )
```

```python
import functools

import jax
import jax.numpy as jnp
from jax import lax
from jax.experimental import pallas as pl
from jax.experimental.pallas import tpu as pltpu
from jax.sharding import PartitionSpec as P

MESH = pl.DeviceIdType.MESH
CORES = 2
PIECE = 256


def gather_encode(
    n_row, n_col, tokens, dec_bias, enc_rows, bias_rows, enc_cols, bias_cols,
    rows_out, cols_out,
    tok, cent, w_rows, w_cols, shift, b_rows, b_cols, w_sem, b_sem, own_sem,
    z_send, z_recv, x_send, x_recv, s_send, s_recv,
    rz_send, rz_recv, cx_send, cx_recv, cs_send, cs_recv,
):
    n_x = n_row // CORES
    r, c = lax.axis_index("row"), lax.axis_index("col")
    x, k = r // CORES, r % CORES
    other = 1 - k
    sibling = {"row": x * CORES + other, "col": c}
    n_piece, n_tok, piece = cols_out.shape[1:]

    def z_peer(s):
        return {"row": r, "col": lax.rem(c + s, n_col)}

    def x_peer(t):
        return {"row": lax.rem(x + t, n_x) * CORES + k, "col": c}

    def from_c(s):
        return lax.rem(c + n_col - s, n_col)

    def from_x(t):
        return lax.rem(x + n_x - t, n_x)

    def local(src, dst, sem):
        copy = pltpu.make_async_copy(src, dst, sem)
        copy.start()
        return copy

    def remote(src, dst, send_sem, recv_sem, device):
        copy = pltpu.make_async_remote_copy(
            src_ref=src, dst_ref=dst, send_sem=send_sem, recv_sem=recv_sem,
            device_id=device, device_id_type=MESH,
        )
        copy.start()
        return copy

    def landed(ref, sem):
        pltpu.make_async_copy(ref, ref, sem).wait()

    barrier = pltpu.get_barrier_semaphore()
    for s in range(1, n_col):
        pl.semaphore_signal(barrier, inc=1, device_id=z_peer(s), device_id_type=MESH)
    for t in range(1, n_x):
        pl.semaphore_signal(barrier, inc=1, device_id=x_peer(t), device_id_type=MESH)
    pl.semaphore_signal(barrier, inc=1, device_id=sibling, device_id_type=MESH)

    own = local(tokens, tok.at[k, x, c], own_sem)
    b_copies = [
        local(dec_bias, shift, b_sem.at[0]),
        local(bias_rows, b_rows, b_sem.at[1]),
        local(bias_cols, b_cols, b_sem.at[2]),
    ]
    w_copies = [
        local(enc_cols, w_cols, w_sem.at[0]),
        local(enc_rows, w_rows, w_sem.at[1]),
    ]
    pl.semaphore_wait(barrier, n_col - 1 + n_x - 1 + 1)

    sent = []
    for s in range(1, n_col):
        sent.append(remote(tokens, tok.at[k, x, c], z_send.at[s], z_recv.at[s], z_peer(s)))
    for t in range(1, n_x):
        sent.append(remote(tokens, tok.at[k, x, c], x_send.at[t, 0], x_recv.at[t, 0], x_peer(t)))
    for s in range(1, n_col):
        block = tok.at[k, x, from_c(s)]
        landed(block, z_recv.at[s])
        for t in range(1, n_x):
            sent.append(remote(block, block, x_send.at[t, s], x_recv.at[t, s], x_peer(t)))
    own.wait()
    sent.append(remote(tok.at[k, x], tok.at[k, x], s_send.at[0], s_recv.at[0], sibling))
    for copy in b_copies:
        copy.wait()
    shift_row = shift[...].astype(jnp.float32).reshape(1, -1)

    def centre(kk, xx):
        raw = tok[kk, xx].astype(jnp.float32).reshape(cent.shape[2:])
        cent[kk, xx] = (raw - shift_row).astype(jnp.bfloat16)

    centre(k, x)
    for t in range(1, n_x):
        for s in range(n_col):
            landed(tok.at[k, from_x(t), from_c(s)], x_recv.at[t, s])
        plane = tok.at[k, from_x(t)]
        sent.append(remote(plane, plane, s_send.at[t], s_recv.at[t], sibling))
    for t in range(1, n_x):
        centre(k, from_x(t))
    for t in range(n_x):
        landed(tok.at[other, from_x(t)], s_recv.at[t])
        centre(other, from_x(t))

    def encode(weight, bias):
        total = jnp.dot(
            cent[...].reshape(n_tok, -1), weight, preferred_element_type=jnp.float32
        )
        return jax.nn.relu(total + bias).astype(jnp.bfloat16)

    row_bias = b_rows[...].astype(jnp.float32).reshape(1, -1)
    col_bias = b_cols[...].astype(jnp.float32).reshape(1, -1)
    w_copies[0].wait()
    for p in range(n_piece):
        at = slice(p * piece, (p + 1) * piece)
        cols_out[r, p] = encode(w_cols[:, at], col_bias[:, at])
        mine = cols_out.at[r, p]
        for t in range(1, n_x):
            sent.append(remote(mine, mine, cx_send.at[t, p], cx_recv.at[t, p], x_peer(t)))
        sent.append(remote(mine, mine, cs_send.at[0, p], cs_recv.at[0, p], sibling))
        if p == 0:
            w_copies[1].wait()
            rows_out[c] = encode(w_rows[...], row_bias).astype(jnp.float32).T.astype(jnp.bfloat16)
            for s in range(1, n_col):
                sent.append(
                    remote(rows_out.at[c], rows_out.at[c], rz_send.at[s], rz_recv.at[s], z_peer(s))
                )
    for p in range(n_piece):
        for t in range(1, n_x):
            theirs = cols_out.at[from_x(t) * CORES + k, p]
            landed(theirs, cx_recv.at[t, p])
            sent.append(remote(theirs, theirs, cs_send.at[t, p], cs_recv.at[t, p], sibling))

    for s in range(1, n_col):
        landed(rows_out.at[from_c(s)], rz_recv.at[s])
    for t in range(n_x):
        for p in range(n_piece):
            landed(cols_out.at[from_x(t) * CORES + other, p], cs_recv.at[t, p])
    for copy in sent:
        copy.wait_send()


def slab_kernel(scale, rows, cols, out, held, sem):
    n_col, row_width, _ = rows.shape
    n_row, n_piece, _, piece = cols.shape

    def copy(b):
        at = pl.ds(pl.multiple_of(b * row_width, row_width), row_width)
        return pltpu.make_async_copy(held.at[b], out.at[at], sem.at[b])

    @pl.loop(0, n_col)
    def _(b):
        for i in range(n_row):
            for p in range(n_piece):
                first = (i * n_piece + p) * piece
                total = jnp.dot(rows[b], cols[i, p], preferred_element_type=jnp.float32)
                held[b, :, first:first + piece] = (total * scale).astype(jnp.bfloat16)
        copy(b).start()

    @pl.loop(0, n_col)
    def _(b):
        copy(b).wait()


def on_device(n_row, n_col, tokens, dec_bias, enc_rows, bias_rows, enc_cols, bias_cols):
    block, width = tokens.shape
    n_tok = block * n_row * n_col
    n_x = n_row // CORES
    row_width, col_width = enc_rows.shape[1], enc_cols.shape[1]
    piece = min(PIECE, col_width)
    n_piece = col_width // piece
    out_bytes = 2 * n_tok * (n_col * row_width + n_row * col_width)
    dma = pltpu.SemaphoreType.DMA
    vmem = pl.BlockSpec(memory_space=pltpu.VMEM)
    anywhere = pl.BlockSpec(memory_space=pltpu.HBM)
    rows, cols = pl.pallas_call(
        functools.partial(gather_encode, n_row, n_col),
        out_shape=(
            pltpu.VMEM((n_col, row_width, n_tok), jnp.bfloat16),
            pltpu.VMEM((n_row, n_piece, n_tok, piece), jnp.bfloat16),
        ),
        in_specs=[anywhere] * 6,
        out_specs=(vmem, vmem),
        scratch_shapes=[
            pltpu.VMEM((CORES, n_x, n_col, block, width), jnp.bfloat16),
            pltpu.VMEM((CORES, n_x, n_col * block, width), jnp.bfloat16),
            pltpu.VMEM((width, row_width), jnp.bfloat16),
            pltpu.VMEM((width, col_width), jnp.bfloat16),
            pltpu.VMEM((width,), jnp.bfloat16),
            pltpu.VMEM((row_width,), jnp.bfloat16),
            pltpu.VMEM((col_width,), jnp.bfloat16),
            dma((2,)),
            dma((3,)),
            dma,
            dma((n_col,)),
            dma((n_col,)),
            dma((n_x, n_col)),
            dma((n_x, n_col)),
            dma((n_x,)),
            dma((n_x,)),
            dma((n_col,)),
            dma((n_col,)),
            dma((n_x, n_piece)),
            dma((n_x, n_piece)),
            dma((n_x, n_piece)),
            dma((n_x, n_piece)),
        ],
        compiler_params=pltpu.CompilerParams(
            collective_id=0, has_side_effects=True, vmem_limit_bytes=57 * 2**20 - out_bytes
        ),
        name="gather_encode",
    )(
        tokens, dec_bias, enc_rows, bias_rows, enc_cols, bias_cols
    )
    return pl.pallas_call(
        functools.partial(slab_kernel, 1.0 / n_tok),
        out_shape=jax.ShapeDtypeStruct((n_col * row_width, n_row * col_width), jnp.bfloat16),
        in_specs=[vmem, vmem],
        out_specs=anywhere,
        scratch_shapes=[
            pltpu.VMEM((n_col, row_width, n_row * col_width), jnp.bfloat16),
            dma((n_col,)),
        ],
        compiler_params=pltpu.CompilerParams(vmem_limit_bytes=40 * 2**20),
        name="slab",
    )(rows, cols)


def solution(mesh):
    in_specs = (
        P(("grp", "row", "col"), None),
        P(),
        P(None, ("row", "col")),
        P(("row", "col")),
        P(None, ("col", "row")),
        P(("col", "row")),
    )
    out_specs = P(("grp", "row"), "col")
    return jax.shard_map(
        functools.partial(on_device, mesh.shape["row"], mesh.shape["col"]),
        mesh=mesh, in_specs=in_specs, out_specs=out_specs, check_vma=False,
    )
```
